32 devices in a mesh: gx: 4 (over z), yz: 8 (over y, x, core).
Axes of the slice: x: 2, y: 2, z: 4, core: 2. Of those that a mesh axis runs over, the one named last changes fastest.
Arguments:
- states_in: bfloat16 [256, 18432], P(None, 'gx'), may hold values from -80 to 80
- norm_gain: float32 [18432], P('gx'), may hold values from 0.1 to 1.9
- w_query: bfloat16 [18432, 12288], P('gx', 'yz'), may hold values from -0.046875 to 0.046875
- w_keyval: bfloat16 [18432, 512], P('gx', 'yz'), may hold values from -0.046875 to 0.046875
- w_out: bfloat16 [12288, 18432], P('yz', 'gx'), may hold values from -0.4375 to 0.4375
- key_cache: bfloat16 [256, 2048, 256], P(('gx', 'yz')), may hold values from -128 to 128
- value_cache: bfloat16 [256, 2048, 256], P(('gx', 'yz')), may hold values from -6 to 6
- lengths: int32 [256], P(('gx', 'yz')), may hold values from 1 to 2048, as said below
- positions: int32 [256], replicated, may hold values from 1 to 4095, as said below
Outputs:
- states: bfloat16 [2, 256, 18432], P(None, 'yz', 'gx')
- new_kv: bfloat16 [2, 256, 512], P(None, ('gx', 'yz'))
The draws below stay inside these ranges and needn't reach their ends.
Inputs may be any that keep to these rules, and one draw needn't show every extreme that they name: `lengths`: at least one row has exactly 2048 valid slots. positions[b] >= lengths[b]; the token of step t stands at positions[b] + t.
All inputs are finite; a program needn't handle non-finite values.
Results may differ from the reference program's by a relative error of at most 0.025.
Values may be sent and summed in bfloat16 or wider, within the bound.
A program may use at most 128 MiB of HBM per device.

```python
import math
import jax
import jax.numpy as jnp
from jax import lax

D = 18432
H = 48
DH = 256
S = 2048
STEPS = 2
ROWS = 256


def row_lengths(key):
    base_key, shift_key, pick_key = jax.random.split(key, 3)
    base = jax.random.randint(base_key, (ROWS,), 8, S + 1)
    shifts = jax.random.randint(shift_key, (ROWS,), 0, 4)
    result = jnp.maximum(jnp.right_shift(base, shifts), 1)
    chosen = jax.random.randint(pick_key, (), 0, ROWS)
    return result.at[chosen].set(S)


def draw_lengths(key, part):
    return row_lengths(key)


def draw_positions(key, part):
    result = row_lengths(key)
    key = jax.random.fold_in(key, 41)
    return result + jax.random.randint(key, (ROWS,), 0, S)


def draw_states_in(key, part):
    key = jax.random.fold_in(key, 11)
    base_key, row_key, block_key = jax.random.split(key, 3)
    column = jnp.arange(D)
    blocks = (D + 127) // 128
    block_scale = jnp.exp(jax.random.uniform(block_key, (blocks,), minval=math.log(0.3), maxval=math.log(3.0)))
    rising = jnp.exp((column.astype(jnp.float32) / D - 0.5) * math.log(3.0))
    base = jax.random.truncated_normal(base_key, -4.0, 4.0, (ROWS, D))
    row_scale = jnp.exp(jax.random.uniform(row_key, (ROWS, 1), minval=math.log(0.3), maxval=math.log(3.0)))
    values = base * row_scale * block_scale[column // 128] * rising
    return values.astype(jnp.bfloat16)


def draw_key_cache(key, part):
    key = jax.random.fold_in(key, 23)
    base_key = jax.random.fold_in(key, 1)
    values = jax.random.truncated_normal(base_key, -6.0, 6.0, (ROWS, S, DH))
    return values.astype(jnp.bfloat16)


def level_of(stream_key, extent, cuts, smallest, top_value):
    level, own = 1.0, jax.random.fold_in(stream_key, 6)
    for axis_at, shards_of in cuts:
        draws = jnp.exp(jax.random.uniform(jax.random.fold_in(own, axis_at), (shards_of,), jnp.float32, smallest / len(cuts), top_value / len(cuts)))
        level = level * jnp.repeat(draws, extent[axis_at] // shards_of).reshape([-1 if axis == axis_at else 1 for axis in range(len(extent))])
    return level


def scatter_about(key, dims, scale, bound, shards=(), held_as=jnp.bfloat16):
    entries = jax.random.normal(key, dims, jnp.float32) * scale
    if len(shards) > 0:
        entries = level_of(key, dims, shards, -0.22, 0.18) * entries
    return jnp.clip(entries, min=-bound, max=bound).astype(held_as)


def setup_inputs(seed: int = 0) -> dict:
    streams_of = jax.random.split(jax.random.key(seed), 10)
    states_in = draw_states_in(jax.random.fold_in(streams_of[9], 71), 0)
    norm_gain = jnp.clip(1.0 + 0.18 * jax.random.normal(streams_of[1], (D,), jnp.float32), 0.1, 1.9)
    w_query = scatter_about(streams_of[2], (D, H * DH), D ** -0.5, 0.046875, ((0, 4), (1, 8)))
    w_keyval = scatter_about(streams_of[3], (D, 2 * DH), D ** -0.5, 0.046875, ((0, 4), (1, 8)))
    w_out = scatter_about(streams_of[4], (H * DH, D), (H * DH // 64) ** -0.5, 0.4375, ((0, 8), (1, 4)))
    key_cache = draw_key_cache(jax.random.fold_in(streams_of[9], 71), 0)
    value_cache = scatter_about(streams_of[6], (ROWS, S, DH), 1.0, 6.0, ((0, 32),))
    lengths = draw_lengths(jax.random.fold_in(streams_of[9], 71), 0)
    positions = draw_positions(jax.random.fold_in(streams_of[9], 71), 0)
    return {"states_in": states_in, "norm_gain": norm_gain, "w_query": w_query, "w_keyval": w_keyval, "w_out": w_out, "key_cache": key_cache, "value_cache": value_cache, "lengths": lengths, "positions": positions}


epsilon = 1e-06
floor_score = -1e+30

def rotary(vectors, places):
    half_width = vectors.shape[-1] // 2
    frequency = jnp.exp(jnp.arange(half_width, dtype=jnp.float32) * (-2.0 * math.log(10000.0) / vectors.shape[-1]))
    angles = places.astype(jnp.float32)[..., None] * frequency
    cosine = jnp.cos(angles)
    sine_part = jnp.sin(angles)
    leading = vectors[..., :half_width]
    trailing = vectors[..., half_width:]
    return jnp.concatenate([leading * cosine - trailing * sine_part, trailing * cosine + leading * sine_part], axis=-1)

def layer_norm(hidden, norm_gain):
    values = hidden.astype(jnp.float32)
    center = lax.optimization_barrier(jnp.mean(values, axis=1, keepdims=True))
    offset = values - center
    spread = lax.optimization_barrier(jnp.mean(offset * offset, axis=1, keepdims=True))
    return (offset * lax.rsqrt(spread + epsilon) * norm_gain).astype(jnp.bfloat16)

def attend_row(inputs):
    queries, cached_keys, cached_values, length, extra_keys, extra_values = inputs
    score_scale = 1.0 / math.sqrt(queries.shape[-1])
    query_float = queries.astype(jnp.float32)
    scores = jnp.einsum('hd,sd->hs', query_float, cached_keys.astype(jnp.float32)) * score_scale
    usable = jnp.arange(cached_keys.shape[0]) < length
    scores = jnp.where(usable[None, :], scores, floor_score)
    extra_scores = jnp.einsum('hd,td->ht', query_float, extra_keys.astype(jnp.float32)) * score_scale
    row_top = jnp.maximum(lax.optimization_barrier(jnp.max(scores, axis=1)), lax.optimization_barrier(jnp.max(extra_scores, axis=1)))[:, None]
    cached_weights = jnp.exp(scores - row_top)
    extra_weights = jnp.exp(extra_scores - row_top)
    weight_sum = lax.optimization_barrier(jnp.sum(cached_weights, axis=1)) + lax.optimization_barrier(jnp.sum(extra_weights, axis=1))
    cached_rounded = lax.optimization_barrier(cached_weights.astype(jnp.bfloat16)).astype(jnp.float32)
    extra_rounded = lax.optimization_barrier(extra_weights.astype(jnp.bfloat16)).astype(jnp.float32)
    weighted = jnp.einsum('hs,sd->hd', cached_rounded, cached_values.astype(jnp.float32))
    weighted = weighted + jnp.einsum('ht,td->hd', extra_rounded, extra_values.astype(jnp.float32))
    return (weighted / weight_sum[:, None]).astype(jnp.bfloat16)

def reference(states_in, norm_gain, w_query, w_keyval, w_out, key_cache, value_cache, lengths, positions):
    total_rows = states_in.shape[0]
    hidden = states_in
    new_keys = []
    new_values = []
    outputs = []
    for step_index in range(STEPS):
        normed = layer_norm(hidden, norm_gain)
        query_sum = jnp.dot(normed, w_query, preferred_element_type=jnp.float32).reshape(total_rows, H, DH)
        queries = rotary(query_sum, positions[:, None] + step_index).astype(jnp.bfloat16)
        keyval = lax.optimization_barrier(jnp.dot(normed, w_keyval, preferred_element_type=jnp.float32).astype(jnp.bfloat16))
        key_new = rotary(keyval[:, :DH].astype(jnp.float32), positions + step_index).astype(jnp.bfloat16)
        new_keys.append(key_new)
        new_values.append(keyval[:, DH:])
        attended = lax.map(attend_row, (queries, key_cache, value_cache, lengths, jnp.stack(new_keys, axis=1), jnp.stack(new_values, axis=1)))
        projected = jnp.dot(attended.reshape(total_rows, H * DH), w_out, preferred_element_type=jnp.float32)
        hidden = (hidden.astype(jnp.float32) + projected).astype(jnp.bfloat16)
        outputs.append(hidden)
    new_kv = jnp.stack([jnp.concatenate([key_part, value_part], axis=1) for key_part, value_part in zip(new_keys, new_values)])
    return (jnp.stack(outputs), new_kv)
```

```python
import functools
import math

import jax
import jax.numpy as jnp
import numpy as np
from jax import lax
from jax.experimental import pallas as pl
from jax.experimental.pallas import tpu as pltpu
from jax.sharding import PartitionSpec as P

D = 18432
DH = 256
STEPS = 2
MESH = pl.DeviceIdType.MESH
VMEM_LIMIT = 48 * 1024 * 1024

epsilon = 1e-06
floor_score = -1e30
frequencies = np.exp(np.arange(DH // 2) * (-2.0 * math.log(10000.0) / DH)).astype(np.float32)


def params(collective_id):
    return pltpu.CompilerParams(
        collective_id=collective_id, has_side_effects=True, vmem_limit_bytes=VMEM_LIMIT
    )


def greet(targets):
    barrier = pltpu.get_barrier_semaphore()
    for target in targets:
        pl.semaphore_signal(barrier, inc=1, device_id=target, device_id_type=MESH)
    pl.semaphore_wait(barrier, len(targets))


def send(src, dst, send_sem, recv_sem, target):
    return pltpu.make_async_remote_copy(
        src_ref=src,
        dst_ref=dst,
        send_sem=send_sem,
        recv_sem=recv_sem,
        device_id=target,
        device_id_type=MESH,
    )


def turn(vectors, cosine, sine_part):
    leading = vectors[..., : DH // 2]
    trailing = vectors[..., DH // 2 :]
    return jnp.concatenate(
        [leading * cosine - trailing * sine_part, trailing * cosine + leading * sine_part], axis=-1
    )


def angles_of(places):
    angles = places.astype(jnp.float32)[..., None] * jnp.asarray(frequencies)
    return jnp.cos(angles), jnp.sin(angles)


def share_kernel(n, x_ref, out_ref, send_sem, recv_sem):
    me = lax.axis_index("gx")
    others = [lax.rem(me + k, n) for k in range(1, n)]
    greet([{"gx": other} for other in others])
    out_ref[me] = x_ref[...]
    copies = [
        send(x_ref, out_ref.at[me], send_sem.at[k], recv_sem.at[k], {"gx": other})
        for k, other in enumerate(others)
    ]
    for copy in copies:
        copy.start()
    for copy in copies:
        copy.wait()


def share(x, n):
    return pl.pallas_call(
        functools.partial(share_kernel, n),
        out_shape=jax.ShapeDtypeStruct((n,) + x.shape, x.dtype),
        in_specs=[pl.BlockSpec(memory_space=pltpu.VMEM)],
        out_specs=pl.BlockSpec(memory_space=pltpu.VMEM),
        scratch_shapes=[pltpu.SemaphoreType.DMA((n - 1,)), pltpu.SemaphoreType.DMA((n - 1,))],
        compiler_params=params(1),
    )(x)


def layer_norm(hidden, norm_gain, n):
    values = hidden.astype(jnp.float32)
    width = values.shape[1]
    mean_here = jnp.sum(values, axis=1) / width
    offset = values - mean_here[:, None]
    square_here = jnp.sum(offset * offset, axis=1)
    both = jnp.concatenate(
        [mean_here[None], square_here[None], jnp.zeros((6, values.shape[0]), jnp.float32)]
    )
    every = share(both, n)
    means, squares = every[:, 0], every[:, 1]
    center = jnp.sum(means, axis=0) / n
    shift = means - center[None]
    spread = (jnp.sum(squares, axis=0) + width * jnp.sum(shift * shift, axis=0)) / (width * n)
    return ((values - center[:, None]) * lax.rsqrt(spread + epsilon)[:, None] * norm_gain).astype(
        jnp.bfloat16
    )


def project_kernel(
    ng, ny, heads, rows, x_ref, wq_ref, wkv_ref, cos_ref, sin_ref, out_ref,
    own, pair_out, pair_in, far_in, kv_own, kv_pair_out, kv_pair_in, kv_far_in, stage, second, third,
    pair_send, pair_recv, far_send, far_recv,
    kv_pair_send, kv_pair_recv, kv_far_send, kv_far_recv, a2a_send_sem, a2a_recv_sem,
):
    step = pl.program_id(0)
    g = lax.axis_index("gx")
    y = lax.axis_index("yz")
    block = rows * ny
    half = ng // 2
    side = lax.rem(g, 2)
    group = g // 2
    partner = g + 1 - 2 * side
    groups = [lax.rem(group + k, half) for k in range(1, half)]
    y_others = [lax.rem(y + k, ny) for k in range(1, ny)]

    @pl.when(step == 0)
    def _():
        greet(
            [{"gx": partner}]
            + [{"gx": 2 * other + side} for other in groups]
            + [{"yz": other} for other in y_others]
        )

    def pair_copy(j):
        return send(pair_out.at[j], pair_in.at[j], pair_send.at[j], pair_recv.at[j], {"gx": partner})

    def far_copies(j):
        return [
            send(own.at[j, other], far_in.at[j, k], far_send.at[j, k], far_recv.at[j, k], {"gx": 2 * other + side})
            for k, other in enumerate(groups)
        ]

    def kv_pair_copy():
        return send(kv_pair_out, kv_pair_in, kv_pair_send, kv_pair_recv, {"gx": partner})

    def kv_far_copies():
        return [
            send(kv_own.at[other], kv_far_in.at[k], kv_far_send.at[k], kv_far_recv.at[k], {"gx": 2 * other + side})
            for k, other in enumerate(groups)
        ]

    def combine(j):
        pair_copy(j).wait()
        own[j] = own[j] + pair_in[j]
        for copy in far_copies(j):
            copy.start()

    product = jnp.dot(x_ref[...], wq_ref[...], preferred_element_type=jnp.float32)
    product = product.reshape(half, 2, block, DH)
    own[step] = jnp.where(side == 0, product[:, 0], product[:, 1])
    pair_out[step] = jnp.where(side == 0, product[:, 1], product[:, 0])
    pair_copy(step).start()

    @pl.when(step == 0)
    def _():
        small = jnp.dot(x_ref[...], wkv_ref[...], preferred_element_type=jnp.float32)
        small = jnp.concatenate(
            [small, jnp.zeros((small.shape[0], 128 - small.shape[1]), jnp.float32)], axis=1
        ).reshape(half, 2, block, 128)
        kv_own[...] = jnp.where(side == 0, small[:, 0], small[:, 1])
        kv_pair_out[...] = jnp.where(side == 0, small[:, 1], small[:, 0])
        kv_pair_copy().start()
        stage[...] = jnp.zeros_like(stage)

    @pl.when(step > 0)
    def _():
        combine(step - 1)

    @pl.when(step == heads - 1)
    def _():
        kv_pair_copy().wait()
        kv_own[...] = kv_own[...] + kv_pair_in[...]
        for copy in kv_far_copies():
            copy.start()
        combine(step)
        for j in range(heads):
            total = own[j, group]
            for k, copy in enumerate(far_copies(j)):
                copy.wait()
                total = total + far_in[j, k]
            turned = turn(total, cos_ref[...], sin_ref[...])
            stage[:, j * rows : (j + 1) * rows, :] = turned.reshape(ny, rows, DH)
        total = kv_own[group]
        for k, copy in enumerate(kv_far_copies()):
            copy.wait()
            total = total + kv_far_in[k]
        stage[:, heads * rows : (heads + 1) * rows, :128] = total.reshape(ny, rows, 128)
        second[...] = stage[...].astype(jnp.bfloat16)
        copies = [
            send(second.at[other], third.at[y], a2a_send_sem.at[k], a2a_recv_sem.at[k], {"yz": other})
            for k, other in enumerate(y_others)
        ]
        for copy in copies:
            copy.start()
        third[y] = second[y]
        for copy in copies:
            copy.wait()
        out_ref[...] = third[...]


def project(normed, w_query, w_keyval, cosine, sine_part, ng, ny, rows):
    total_rows, depth = normed.shape
    heads = w_query.shape[1] // DH
    narrow = w_keyval.shape[1]
    slots = (heads + 2) // 2 * 2
    block = rows * ny
    half = ng // 2
    dma = pltpu.SemaphoreType.DMA
    whole = lambda j: (0, 0)
    return pl.pallas_call(
        functools.partial(project_kernel, ng, ny, heads, rows),
        grid=(heads,),
        out_shape=jax.ShapeDtypeStruct((ny, slots * rows, DH), jnp.bfloat16),
        in_specs=[
            pl.BlockSpec((total_rows, depth), whole),
            pl.BlockSpec((depth, DH), lambda j: (0, j)),
            pl.BlockSpec((depth, narrow), whole),
            pl.BlockSpec((block, DH // 2), whole),
            pl.BlockSpec((block, DH // 2), whole),
        ],
        out_specs=pl.BlockSpec(memory_space=pltpu.VMEM),
        scratch_shapes=[
            pltpu.VMEM((heads, half, block, DH), jnp.float32),
            pltpu.VMEM((heads, half, block, DH), jnp.float32),
            pltpu.VMEM((heads, half, block, DH), jnp.float32),
            pltpu.VMEM((heads, half - 1, block, DH), jnp.float32),
            pltpu.VMEM((half, block, 128), jnp.float32),
            pltpu.VMEM((half, block, 128), jnp.float32),
            pltpu.VMEM((half, block, 128), jnp.float32),
            pltpu.VMEM((half - 1, block, 128), jnp.float32),
            pltpu.VMEM((ny, slots * rows, DH), jnp.float32),
            pltpu.VMEM((ny, slots * rows, DH), jnp.bfloat16),
            pltpu.VMEM((ny, slots * rows, DH), jnp.bfloat16),
            dma((heads,)),
            dma((heads,)),
            dma((heads, half - 1)),
            dma((heads, half - 1)),
            dma,
            dma,
            dma((half - 1,)),
            dma((half - 1,)),
            dma((ny - 1,)),
            dma((ny - 1,)),
        ],
        compiler_params=params(2),
    )(normed, w_query, w_keyval, cosine, sine_part)


def spread_kernel(ng, ny, x_ref, out_ref, send_sem, recv_sem):
    g = lax.axis_index("gx")
    y = lax.axis_index("yz")
    pairs = [(a, b) for a in range(ng) for b in range(ny) if a or b]
    places = [(lax.rem(g + a, ng), lax.rem(y + b, ny)) for a, b in pairs]
    greet([{"gx": to_g, "yz": to_y} for to_g, to_y in places])
    copies = [
        send(x_ref.at[to_y], out_ref.at[g, y], send_sem.at[k], recv_sem.at[k], {"gx": to_g, "yz": to_y})
        for k, (to_g, to_y) in enumerate(places)
    ]
    for copy in copies:
        copy.start()
    out_ref[g, y] = x_ref[y]
    for copy in copies:
        copy.wait()


def spread_heads(x, ng, ny):
    count = ng * ny - 1
    return pl.pallas_call(
        functools.partial(spread_kernel, ng, ny),
        out_shape=jax.ShapeDtypeStruct((ng,) + x.shape, x.dtype),
        in_specs=[pl.BlockSpec(memory_space=pltpu.VMEM)],
        out_specs=pl.BlockSpec(memory_space=pltpu.VMEM),
        scratch_shapes=[pltpu.SemaphoreType.DMA((count,)), pltpu.SemaphoreType.DMA((count,))],
        compiler_params=params(3),
    )(x)


def output_kernel(
    n, chunks, width, x_ref, w_ref, h_ref, out_ref,
    own, pair_out, pair_in, far_in, pair_send, pair_recv, far_send, far_recv,
):
    step = pl.program_id(0)
    me = lax.axis_index("yz")
    half = n // 2
    side = lax.rem(me, 2)
    group = me // 2
    partner = me + 1 - 2 * side
    groups = [lax.rem(group + k, half) for k in range(1, half)]
    rows = h_ref.shape[0]

    @pl.when(step == 0)
    def _():
        greet([{"yz": partner}] + [{"yz": 2 * other + side} for other in groups])

    def pair_copy(s):
        return send(pair_out.at[s], pair_in.at[s], pair_send.at[s], pair_recv.at[s], {"yz": partner})

    def far_copies(s):
        return [
            send(own.at[s, other], far_in.at[s, k], far_send.at[s, k], far_recv.at[s, k], {"yz": 2 * other + side})
            for k, other in enumerate(groups)
        ]

    def combine(s):
        pair_copy(s).wait()
        own[s] = own[s] + pair_in[s]
        for copy in far_copies(s):
            copy.start()

    product = jnp.dot(x_ref[...], w_ref[...], preferred_element_type=jnp.float32)
    product = product.reshape(half, 2, rows, width)
    own[step] = jnp.where(side == 0, product[:, 0], product[:, 1])
    pair_out[step] = jnp.where(side == 0, product[:, 1], product[:, 0])
    pair_copy(step).start()

    @pl.when(step > 0)
    def _():
        combine(step - 1)

    @pl.when(step == chunks - 1)
    def _():
        combine(step)
        for s in range(chunks):
            total = own[s, group]
            for k, copy in enumerate(far_copies(s)):
                copy.wait()
                total = total + far_in[s, k]
            columns = slice(s * width, (s + 1) * width)
            out_ref[:, columns] = (h_ref[:, columns].astype(jnp.float32) + total).astype(jnp.bfloat16)


def output(x, w_out, own_rows, n):
    total_rows, depth = x.shape
    rows, columns = own_rows.shape
    width = 768
    chunks = columns // width
    half = n // 2
    dma = pltpu.SemaphoreType.DMA
    return pl.pallas_call(
        functools.partial(output_kernel, n, chunks, width),
        grid=(chunks,),
        out_shape=jax.ShapeDtypeStruct((rows, columns), jnp.bfloat16),
        in_specs=[
            pl.BlockSpec((total_rows, depth), lambda j: (0, 0)),
            pl.BlockSpec((depth, width), lambda j: (0, j)),
            pl.BlockSpec((rows, columns), lambda j: (0, 0)),
        ],
        out_specs=pl.BlockSpec(memory_space=pltpu.VMEM),
        scratch_shapes=[
            pltpu.VMEM((chunks, half, rows, width), jnp.float32),
            pltpu.VMEM((chunks, half, rows, width), jnp.float32),
            pltpu.VMEM((chunks, half, rows, width), jnp.float32),
            pltpu.VMEM((chunks, half - 1, rows, width), jnp.float32),
            dma((chunks,)),
            dma((chunks,)),
            dma((chunks, half - 1)),
            dma((chunks, half - 1)),
        ],
        compiler_params=params(4),
    )(x, w_out, own_rows)


def gather_kernel(n, x_ref, out_ref, send_sem, recv_sem, pair_send, pair_recv):
    me = lax.axis_index("yz")
    half = n // 2
    side = lax.rem(me, 2)
    group = me // 2
    partner = me + 1 - 2 * side
    groups = [lax.rem(group + k, half) for k in range(1, half)]
    greet([{"yz": partner}] + [{"yz": 2 * other + side} for other in groups])
    copies = [
        send(x_ref, out_ref.at[me], send_sem.at[k], recv_sem.at[k], {"yz": 2 * other + side})
        for k, other in enumerate(groups)
    ]
    for copy in copies:
        copy.start()
    passed = [send(x_ref, out_ref.at[me], pair_send.at[half - 1], pair_recv.at[half - 1], {"yz": partner})]
    passed[0].start()
    out_ref[me] = x_ref[...]
    for k, copy in enumerate(copies):
        copy.wait_recv()
        source = 2 * lax.rem(group + half - 1 - k, half) + side
        passed.append(
            send(out_ref.at[source], out_ref.at[source], pair_send.at[k], pair_recv.at[k], {"yz": partner})
        )
        passed[-1].start()
    for copy in copies:
        copy.wait_send()
    for copy in passed:
        copy.wait()


def gather(x, n):
    half = n // 2
    dma = pltpu.SemaphoreType.DMA
    return pl.pallas_call(
        functools.partial(gather_kernel, n),
        out_shape=jax.ShapeDtypeStruct((n,) + x.shape, x.dtype),
        in_specs=[pl.BlockSpec(memory_space=pltpu.VMEM)],
        out_specs=pl.BlockSpec(memory_space=pltpu.VMEM),
        scratch_shapes=[dma((half - 1,)), dma((half - 1,)), dma((half,)), dma((half,))],
        compiler_params=params(5),
    )(x)


def attend(queries, key_cache, value_cache, lengths, extra_keys, extra_values):
    score_scale = 1.0 / math.sqrt(queries.shape[-1])
    extra_scores = (
        jnp.einsum("rhd,rtd->rht", queries, extra_keys, preferred_element_type=jnp.float32)
        * score_scale
    )
    scores = (
        jnp.einsum("rhd,rsd->rhs", queries, key_cache, preferred_element_type=jnp.float32)
        * score_scale
    )
    usable = jnp.arange(key_cache.shape[1])[None, :] < lengths[:, None]
    scores = jnp.where(usable[:, None, :], scores, floor_score)
    row_top = jnp.maximum(jnp.max(scores, axis=2), jnp.max(extra_scores, axis=2))[..., None]
    cached_weights = jnp.exp(scores - row_top)
    extra_weights = jnp.exp(extra_scores - row_top)
    weight_sum = jnp.sum(cached_weights, axis=2) + jnp.sum(extra_weights, axis=2)
    weighted = jnp.einsum(
        "rhs,rsd->rhd",
        cached_weights.astype(jnp.bfloat16),
        value_cache,
        preferred_element_type=jnp.float32,
    )
    weighted = weighted + jnp.einsum(
        "rht,rtd->rhd",
        extra_weights.astype(jnp.bfloat16),
        extra_values,
        preferred_element_type=jnp.float32,
    )
    return (weighted / weight_sum[..., None]).astype(jnp.bfloat16)


def on_device(
    states_in, norm_gain, w_query, w_keyval, w_out, key_cache, value_cache, lengths, positions
):
    ng = lax.axis_size("gx")
    ny = lax.axis_size("yz")
    g = lax.axis_index("gx")
    y = lax.axis_index("yz")
    rows = key_cache.shape[0]
    total_rows, features = states_in.shape
    block = total_rows // ng
    share_rows = total_rows // ny
    heads = w_query.shape[1] // DH
    own_positions = lax.dynamic_slice_in_dim(positions, (g * ny + y) * rows, rows)
    block_positions = lax.dynamic_slice_in_dim(positions, g * block, block)
    own_rows = lax.dynamic_slice_in_dim(states_in, y * share_rows, share_rows, 0)
    hidden = states_in
    new_keys = []
    new_values = []
    results = []
    for t in range(STEPS):
        normed = layer_norm(hidden, norm_gain, ng)
        cosine, sine_part = angles_of(block_positions + t)
        arrived = project(normed, w_query, w_keyval, cosine, sine_part, ng, ny, rows)
        arrived = arrived.reshape(ny, -1, rows, DH)
        queries = arrived[:, :heads].transpose(2, 0, 1, 3).reshape(rows, ny * heads, DH)
        keyval = arrived[:, heads, :, : w_keyval.shape[1]].transpose(1, 0, 2).reshape(rows, 2 * DH)
        key_new = turn(keyval[:, :DH].astype(jnp.float32), *angles_of(own_positions + t)).astype(
            jnp.bfloat16
        )
        new_keys.append(key_new)
        new_values.append(keyval[:, DH:])
        attended = attend(
            queries,
            key_cache,
            value_cache,
            lengths,
            jnp.stack(new_keys, axis=1),
            jnp.stack(new_values, axis=1),
        )
        parcels = attended.reshape(rows, ny, 2, heads * DH // 2).transpose(1, 0, 2, 3)
        spread = spread_heads(parcels.reshape(ny, 2 * rows, heads * DH // 2), ng, ny)
        own_rows = output(spread.reshape(total_rows, heads * DH), w_out, own_rows, ny)
        results.append(own_rows)
        if t + 1 < STEPS:
            hidden = gather(own_rows, ny).reshape(total_rows, features)
    new_kv = jnp.stack(
        [
            jnp.concatenate([key_part, value_part], axis=1)
            for key_part, value_part in zip(new_keys, new_values)
        ]
    )
    return (jnp.stack(results), new_kv)


def solution(mesh):
    in_specs = (
        P(None, "gx"),
        P("gx"),
        P("gx", "yz"),
        P("gx", "yz"),
        P("yz", "gx"),
        P(("gx", "yz"), None, None),
        P(("gx", "yz"), None, None),
        P(("gx", "yz")),
        P(),
    )
    out_specs = (P(None, "yz", "gx"), P(None, ("gx", "yz"), None))
    return jax.shard_map(
        on_device, mesh=mesh, in_specs=in_specs, out_specs=out_specs, check_vma=False
    )
```
